32 devices in a mesh: groups: 2 (over x), expert: 16 (over z, y, core).
Axes of the slice: x: 2, y: 2, z: 4, core: 2. Of those that a mesh axis runs over, the one named last changes fastest.
Arguments:
- tokens: bfloat16 [4096, 1536], P(('groups', 'expert')), parts along dimension 0, may hold values from -6 to 6
- target: bfloat16 [4096, 1536], P(('groups', 'expert')), parts along dimension 0, may hold values from -6 to 6
- expert_ids: int32 [4096, 8], P(('groups', 'expert')), parts along dimension 0, may hold values from 0 to 31, all different within a row; in each aligned block of 128 rows (0 to 127, 128 to 255, ...) at most 48 rows name the same one
- gate_weights: float32 [4096, 8], P(('groups', 'expert')), parts along dimension 0, may hold values from 0.05 to 0.5
- w_gate: bfloat16 [32, 1536, 384], P('expert'), may hold values from -0.15625 to 0.15625
- w_up: bfloat16 [32, 1536, 384], P('expert'), may hold values from -0.15625 to 0.15625
- w_down: bfloat16 [32, 384, 1536], P('expert'), may hold values from -0.3125 to 0.3125
- dir_gate: bfloat16 [32, 1536, 384], P('expert'), may hold values from -0.15625 to 0.15625
- dir_up: bfloat16 [32, 1536, 384], P('expert'), may hold values from -0.15625 to 0.15625
- dir_down: bfloat16 [32, 384, 1536], P('expert'), may hold values from -0.3125 to 0.3125
Outputs:
- hv_gate: bfloat16 [64, 1536, 384], P(('groups', 'expert')), parts along dimension 0
- hv_up: bfloat16 [64, 1536, 384], P(('groups', 'expert')), parts along dimension 0
- hv_down: bfloat16 [64, 384, 1536], P(('groups', 'expert')), parts along dimension 0
The draws below stay inside these ranges and needn't reach their ends.
There are 2 independent parts, one for each index of `groups`. The reference program is written for one: setup_inputs(seed, part) draws one part's arguments, and reference() takes and returns one part's arrays. A program takes and returns all parts, laid end to end along the dimension named above; an argument that names none is the same for every part. Nothing has to cross between parts.
Inputs may be any that keep to these rules, and one draw needn't show every extreme that they name: `expert_ids`: each token names 8 different experts. In the rows of one index of expert no expert is named more than 48 times, and in some such rows one expert is named exactly 48 times.
All inputs are finite; a program needn't handle non-finite values.
Results may differ from the reference program's by a relative error of at most 0.0068.
Values may be sent and summed in bfloat16 or wider, within the bound.
No kernel may reach another device: no remote copies, remote signals or barrier semaphores. Data moves between devices by JAX's collectives and lax.ppermute only.
A program may use at most 128 MiB of HBM per device.

```python
import math
import jax
import jax.numpy as jnp
import numpy as np
from jax import lax

D = 1536
FF = 384
TOPK = 8
TOK_DEV = 128
EXPERTS = 32
TOKENS = 2048
CAP = 48
N_EXPERT = 16


def levels(rng, extent, shards, low, high):
    level = 1.0
    for dim, shards_of in shards:
        steps = jax.random.uniform(jax.random.fold_in(jax.random.fold_in(rng, 6), dim), (shards_of,), jnp.float32, low / len(shards), high / len(shards))
        level = level * jnp.repeat(jnp.exp(steps), extent[dim] // shards_of).reshape((-1,) + (1,) * (len(extent) - 1 - dim))
    return level


def shared_out(own_key, own, number, rows, amount, top, reach, skew):
    order = jax.random.permutation(own_key, amount)
    packed, common = shares(amount, rows * top, reach, skew, True), shares(amount, rows * top, reach, skew, False)
    places = jnp.arange(amount)

    def named(tallies, offset_by):
        used = int((tallies > 0).sum())
        fixed = max(1, used // 4)
        shifted = fixed + (places - fixed + offset_by * (used - fixed)) % max(1, amount - fixed)
        return jnp.zeros((amount,), jnp.int32).at[order[jnp.where(places < fixed, places, shifted)]].set(jnp.asarray(tallies, jnp.int32))

    tallies = jnp.where(number % 4 == 0, named(packed, number // 4), named(common, number - number // 4 - 1))
    mixed = jax.random.permutation(jax.random.fold_in(own, 3), amount)
    source_of, taker = mixed[0:amount // 2 * 2:2], mixed[1:amount // 2 * 2:2]
    margin = jnp.minimum(tallies[source_of] - 1, reach - tallies[taker]) // 2
    margin = jnp.where((source_of == order[0]) | (taker == order[0]) | (tallies[taker] == 0), 0, jnp.maximum(margin, 0))
    shifted = jax.random.randint(jax.random.fold_in(own, 4), (amount // 2,), 0, 1 << 20) % (margin + 1)
    tallies = tallies.at[source_of].add(-shifted).at[taker].add(shifted)
    labels = jnp.searchsorted(jnp.cumsum(tallies), jnp.arange(rows * top), side="right").astype(jnp.int32)
    grid = labels.reshape(top, rows).T
    grid = grid[jax.random.permutation(jax.random.fold_in(own, 1), rows)]
    offset_by = jax.random.randint(jax.random.fold_in(own, 2), (rows, 1), 0, top)
    return jnp.take_along_axis(grid, (jnp.arange(top)[None, :] + offset_by) % top, axis=1)


def shares(amount, total, bound, lean, full):
    loads = [(1 << 20) // math.isqrt(standing ** lean) + 1 for standing in range(1, amount + 1)]
    largest = bound if full else min(bound, max(-(-total // amount), total * loads[0] // sum(loads)))
    least = 1 if total - largest >= amount - 1 else 0
    holding, surplus = [largest] + [least] * (amount - 1), total - largest - least * (amount - 1)
    while surplus > 0:
        free = [i for i in range(1, amount) if holding[i] < largest] or [i for i in range(1, amount) if holding[i] < bound]
        pool, budget = sum([loads[i] for i in free]), surplus
        for i in free:
            more = min(bound - holding[i], max(1, budget * loads[i] // pool), surplus)
            holding[i] = holding[i] + more
            surplus = surplus - more
    return np.array(holding)


def centred(key, extent, deviation, limit, pieces=(), kind=jnp.bfloat16):
    gain = levels(key, extent, pieces, -0.22, 0.18) if pieces else 1.0
    drawn = jax.random.normal(key, extent, jnp.float32) * deviation * gain
    return jnp.minimum(jnp.maximum(drawn, -limit), limit).astype(kind)


def setup_inputs(seed: int = 0, part: int = 0) -> dict:
    streams_of = jax.random.split(jax.random.key(seed), 11)
    part_keys = jax.random.split(jax.random.fold_in(streams_of[10], part), 11)
    tokens = centred(part_keys[0], (TOKENS, D), 1.0, 6.0, ((0, 16),))
    target = centred(part_keys[1], (TOKENS, D), 1.0, 6.0, ((0, 16),))
    expert_ids_keys = jax.random.split(jax.random.fold_in(part_keys[2], 1), TOKENS // TOK_DEV)
    expert_ids_turns = jax.random.permutation(jax.random.fold_in(part_keys[2], 3), TOKENS // TOK_DEV)
    expert_ids = jax.vmap(lambda own, number: shared_out(jax.random.fold_in(part_keys[2], 2), own, number, TOK_DEV, EXPERTS, TOPK, CAP, 2))(expert_ids_keys, expert_ids_turns).reshape((TOKENS, TOPK))
    gate_weights = jnp.clip(jnp.exp(math.log(0.5) - 2.3025851 * jax.random.uniform(part_keys[3], (TOKENS, TOPK), jnp.float32) ** levels(part_keys[3], (TOKENS, TOPK), ((0, 16),), -0.2, 0.2)), 0.05, 0.5)
    w_gate = centred(streams_of[4], (EXPERTS, D, FF), D ** -0.5, 0.15625, ((0, 16),))
    w_up = centred(streams_of[5], (EXPERTS, D, FF), D ** -0.5, 0.15625, ((0, 16),))
    w_down = centred(streams_of[6], (EXPERTS, FF, D), FF ** -0.5, 0.3125, ((0, 16),))
    dir_gate = centred(streams_of[7], (EXPERTS, D, FF), D ** -0.5, 0.15625, ((0, 16),))
    dir_up = centred(streams_of[8], (EXPERTS, D, FF), D ** -0.5, 0.15625, ((0, 16),))
    dir_down = centred(streams_of[9], (EXPERTS, FF, D), FF ** -0.5, 0.3125, ((0, 16),))
    return dict(tokens=tokens, target=target, expert_ids=expert_ids, gate_weights=gate_weights, w_gate=w_gate, w_up=w_up, w_down=w_down, dir_gate=dir_gate, dir_up=dir_up, dir_down=dir_down)


def silu_parts(preact):
    sigmoid_value = jax.nn.sigmoid(preact)
    activation = preact * sigmoid_value
    first_deriv = sigmoid_value * (1.0 + preact * (1.0 - sigmoid_value))
    second_deriv = sigmoid_value * (1.0 - sigmoid_value) * (2.0 + preact * (1.0 - 2.0 * sigmoid_value))
    return activation, first_deriv, second_deriv


def slot_index(expert_ids):
    blocks = expert_ids.reshape(N_EXPERT, TOK_DEV * TOPK)
    expert_names = jnp.arange(EXPERTS, dtype=jnp.int32)

    def one_block(block_ids):
        hit_table = (block_ids[:, None] == expert_names[None, :]).astype(jnp.int32)
        return jnp.sum(jnp.cumsum(hit_table, 0) * hit_table, 1) - 1

    position = lax.map(one_block, blocks).reshape(-1)
    route_ids = expert_ids.reshape(-1)
    block_of = jnp.arange(TOKENS * TOPK, dtype=jnp.int32) // (TOK_DEV * TOPK)
    return ((route_ids * N_EXPERT + block_of) * CAP + position).astype(jnp.int32)


def front_part(expert_rows, w_gate, w_up, dir_gate, dir_up):
    pre_gate = jnp.dot(expert_rows, w_gate, preferred_element_type=jnp.float32)
    pre_up = jnp.dot(expert_rows, w_up, preferred_element_type=jnp.float32)
    dot_gate = jnp.dot(expert_rows, dir_gate, preferred_element_type=jnp.float32)
    dot_up = jnp.dot(expert_rows, dir_up, preferred_element_type=jnp.float32)
    activation, first_deriv, second_deriv = silu_parts(pre_gate)
    hidden = (activation * pre_up).astype(jnp.bfloat16)
    hidden_dot = (first_deriv * dot_gate * pre_up + activation * dot_up).astype(jnp.bfloat16)
    return pre_gate, pre_up, dot_gate, dot_up, activation, first_deriv, second_deriv, hidden, hidden_dot


def forward_expert(operands):
    expert_rows, w_gate, w_up, w_down, dir_gate, dir_up, dir_down = operands
    parts = front_part(expert_rows, w_gate, w_up, dir_gate, dir_up)
    hidden, hidden_dot = parts[7], parts[8]
    out = jnp.dot(hidden, w_down, preferred_element_type=jnp.float32).astype(jnp.bfloat16)
    out_dot = (jnp.dot(hidden_dot, w_down, preferred_element_type=jnp.float32)
               + jnp.dot(hidden, dir_down, preferred_element_type=jnp.float32)).astype(jnp.bfloat16)
    return out, out_dot


def backward_expert(operands):
    expert_rows, w_gate, w_up, w_down, dir_gate, dir_up, dir_down, cot, cot_dot = operands
    pre_gate, pre_up, dot_gate, dot_up, activation, first_deriv, second_deriv, hidden, hidden_dot = front_part(
        expert_rows, w_gate, w_up, dir_gate, dir_up)
    grad_hidden = jnp.dot(cot, w_down.T, preferred_element_type=jnp.float32)
    grad_dot = (jnp.dot(cot_dot, w_down.T, preferred_element_type=jnp.float32)
                + jnp.dot(cot, dir_down.T, preferred_element_type=jnp.float32))
    gate_dot = (grad_dot * first_deriv * pre_up + grad_hidden * second_deriv * dot_gate * pre_up
                + grad_hidden * first_deriv * dot_up).astype(jnp.bfloat16)
    up_dot = (grad_dot * activation + grad_hidden * first_deriv * dot_gate).astype(jnp.bfloat16)
    hv_gate = jnp.dot(expert_rows.T, gate_dot, preferred_element_type=jnp.float32).astype(jnp.bfloat16)
    hv_up = jnp.dot(expert_rows.T, up_dot, preferred_element_type=jnp.float32).astype(jnp.bfloat16)
    hv_down = (jnp.dot(hidden_dot.T, cot, preferred_element_type=jnp.float32)
               + jnp.dot(hidden.T, cot_dot, preferred_element_type=jnp.float32)).astype(jnp.bfloat16)
    return hv_gate, hv_up, hv_down


def reference(tokens, target, expert_ids, gate_weights, w_gate, w_up, w_down, dir_gate, dir_up, dir_down):
    slot = slot_index(expert_ids)
    slot_count = EXPERTS * N_EXPERT * CAP
    model_width = tokens.shape[1]

    def to_slots(entries):
        placed = jnp.zeros((slot_count, model_width), jnp.bfloat16).at[slot].set(entries)
        return placed.reshape(EXPERTS, N_EXPERT * CAP, model_width)

    def from_slots(buffer):
        picked = buffer.reshape(slot_count, model_width)[slot]
        return picked.reshape(TOKENS, TOPK, model_width).astype(jnp.float32)

    expert_rows = to_slots(jnp.repeat(tokens, TOPK, axis=0))
    out, out_dot = lax.map(forward_expert, (expert_rows, w_gate, w_up, w_down, dir_gate, dir_up, dir_down))
    merged = jnp.sum(gate_weights[:, :, None] * from_slots(out), 1)
    merged_dot = jnp.sum(gate_weights[:, :, None] * from_slots(out_dot), 1)
    residual = merged - target.astype(jnp.float32)
    cot = to_slots((gate_weights[:, :, None] * residual[:, None, :]).astype(jnp.bfloat16).reshape(-1, model_width))
    cot_dot = to_slots((gate_weights[:, :, None] * merged_dot[:, None, :]).astype(jnp.bfloat16).reshape(-1, model_width))
    hv_gate, hv_up, hv_down = lax.map(backward_expert, (expert_rows, w_gate, w_up, w_down, dir_gate, dir_up, dir_down, cot, cot_dot))
    return (hv_gate, hv_up, hv_down)
```

```python
import functools

import jax
import jax.numpy as jnp
from jax import lax
from jax.experimental import pallas as pl
from jax.experimental.pallas import tpu as pltpu
from jax.sharding import PartitionSpec as P

F32 = jnp.float32
BF16 = jnp.bfloat16
VMEM_LIMIT = 56 * 1024 * 1024
LANES = 128
ANY = pl.BlockSpec(memory_space=pl.ANY)


def dot(a, b):
    return jnp.dot(a, b, preferred_element_type=F32)


def dot_rows(a, b):
    return lax.dot_general(a, b, (((0,), (0,)), ((), ())), preferred_element_type=F32)


def dot_columns(a, b):
    return lax.dot_general(a, b, (((1,), (1,)), ((), ())), preferred_element_type=F32)


class Copies:
    def __init__(self, sems):
        self.sems, self.count = sems, 0

    def start(self, src, dst):
        copy = pltpu.make_async_copy(src, dst, self.sems.at[self.count])
        self.count += 1
        copy.start()
        return copy


def forward_kernel(cfg, own_ref, *refs):
    tok, width, ff, experts, cap, top_k, pieces = cfg
    blocks = refs[: len(pieces)]
    (wg, wu, dg, du, wd, dd) = refs[len(pieces) : len(pieces) + 6]
    outs = refs[len(pieces) + 6 :]
    (near_hbm, far_hbm, rows_hbm, sel_hbm, grad_hbm, hid_hbm) = outs[:6]
    (x, w, wdv, ddv, rows, sel, pre, grad, hid, out, part, sems) = outs[6:]
    copies = Copies(sems)
    n_blocks = sum(pieces) // tok
    per = n_blocks * cap
    at = 0
    x_in = []
    for piece, ref in zip(pieces, blocks):
        x_in.append((at // tok, copies.start(ref, x.at[pl.ds(at, piece)])))
        at += piece
    w_in, d_in = [], []
    for e in range(experts):
        w_in.append(
            [
                copies.start(src.at[e], w.at[e, :, pl.ds(k * ff, ff)])
                for k, src in enumerate((wg, wu, dg, du))
            ]
        )
        d_in.append([copies.start(wd.at[e], wdv.at[e]), copies.start(dd.at[e], ddv.at[e])])

    before = lax.broadcasted_iota(jnp.int32, (tok, tok), 0) < lax.broadcasted_iota(
        jnp.int32, (tok, tok), 1
    )
    before = before.astype(BF16)
    place = lax.broadcasted_iota(jnp.int32, (cap, tok), 0).astype(F32)
    weight = [[] for _ in range(experts)]
    waits = dict(x_in)
    for b in range(n_blocks):
        if b in waits:
            waits[b].wait()
        xb = x[b * tok : (b + 1) * tok, :]
        routes = xb[:, width : width + LANES].astype(F32).T
        ids = routes[0:top_k]
        gates = (routes[top_k : 2 * top_k] + routes[2 * top_k : 3 * top_k]) + routes[
            3 * top_k : 4 * top_k
        ]
        for e in range(experts):
            named = ids == (own_ref[0] + e).astype(F32)
            hit = jnp.sum(jnp.where(named, 1.0, 0.0), axis=0, keepdims=True)
            gate = jnp.sum(jnp.where(named, gates, 0.0), axis=0, keepdims=True)
            rank = dot(jnp.broadcast_to(hit, (8, tok)).astype(BF16), before)[0:1]
            chosen = jnp.where((rank == place) & (hit > 0.0), 1.0, 0.0)
            weight[e].append(jnp.sum(chosen * gate, axis=1, keepdims=True))
            sel[b, e * cap : (e + 1) * cap, :] = chosen.astype(BF16)
        picked = dot(sel[b], xb[:, 0:width]).astype(BF16)
        for e in range(experts):
            rows[e, b * cap : (b + 1) * cap, :] = picked[e * cap : (e + 1) * cap]
    done = [copies.start(rows, rows_hbm), copies.start(sel, sel_hbm)]

    step = 16
    for e in range(experts):
        for c in w_in[e]:
            c.wait()
        pre[e] = dot(rows[e], w[e])
    for e in range(experts):
        g_all = jnp.concatenate(weight[e], axis=0)
        for r in range(0, per, step):
            at = slice(r, r + step)
            g = g_all[at]
            p, u = pre[e, at, 0:ff], pre[e, at, ff : 2 * ff]
            dgv, duv = pre[e, at, 2 * ff : 3 * ff], pre[e, at, 3 * ff :]
            s = jax.nn.sigmoid(p)
            act = g * (p * s)
            slope = g * (s * (1.0 + p * (1.0 - s)))
            curv = g * (s * (1.0 - s) * (2.0 + p * (1.0 - 2.0 * s)))
            slope_up = slope * u
            grad[e, at, 0:ff] = slope_up
            grad[e, at, ff : 2 * ff] = curv * dgv * u + slope * duv
            grad[e, at, 2 * ff : 3 * ff] = act
            grad[e, at, 3 * ff :] = slope * dgv
            hid[e, at, 0:ff] = (act * u).astype(BF16)
            hid[e, at, ff:] = (slope_up * dgv + act * duv).astype(BF16)
        for c in d_in[e]:
            c.wait()
        h, hd = hid[e, :, 0:ff], hid[e, :, ff:]
        o = dot(h, wdv[e]).astype(BF16)
        od = (dot(hd, wdv[e]) + dot(h, ddv[e])).astype(BF16)
        for b in range(n_blocks):
            out[b, e * cap : (e + 1) * cap, 0:width] = o[b * cap : (b + 1) * cap]
            out[b, e * cap : (e + 1) * cap, width:] = od[b * cap : (b + 1) * cap]
    done += [copies.start(grad, grad_hbm), copies.start(hid, hid_hbm)]
    half = n_blocks // 2
    for b in [*range(half, n_blocks), *range(half)]:
        part[b * tok : (b + 1) * tok, :] = dot_rows(sel[b], out[b]).astype(BF16)
        if b == n_blocks - 1:
            done.append(copies.start(part.at[pl.ds(half * tok, half * tok)], far_hbm))
        if b == half - 1:
            done.append(copies.start(part.at[pl.ds(0, half * tok)], near_hbm))
    for c in done:
        c.wait()


def forward(own, pieces, weights, tok, cap, top_k):
    wg, _, wd = weights[0], weights[1], weights[4]
    experts, width, ff = wg.shape
    sizes = tuple(p.shape[0] for p in pieces)
    total = sum(sizes)
    n_blocks = total // tok
    per = n_blocks * cap
    shape = jax.ShapeDtypeStruct
    return pl.pallas_call(
        functools.partial(forward_kernel, (tok, width, ff, experts, cap, top_k, sizes)),
        in_specs=[pl.BlockSpec(memory_space=pltpu.SMEM)] + [ANY] * (len(pieces) + 6),
        out_specs=[ANY] * 6,
        out_shape=[
            shape((total // 2, 2 * width), BF16),
            shape((total // 2, 2 * width), BF16),
            shape((experts, per, width), BF16),
            shape((n_blocks, experts * cap, tok), BF16),
            shape((experts, per, 4 * ff), F32),
            shape((experts, per, 2 * ff), BF16),
        ],
        scratch_shapes=[
            pltpu.VMEM((total, pieces[0].shape[1]), BF16),
            pltpu.VMEM((experts, width, 4 * ff), BF16),
            pltpu.VMEM((experts, ff, width), BF16),
            pltpu.VMEM((experts, ff, width), BF16),
            pltpu.VMEM((experts, per, width), BF16),
            pltpu.VMEM((n_blocks, experts * cap, tok), BF16),
            pltpu.VMEM((experts, per, 4 * ff), F32),
            pltpu.VMEM((experts, per, 4 * ff), F32),
            pltpu.VMEM((experts, per, 2 * ff), BF16),
            pltpu.VMEM((n_blocks, experts * cap, 2 * width), BF16),
            pltpu.VMEM((total, 2 * width), BF16),
            pltpu.SemaphoreType.DMA((len(pieces) + 6 * experts + 6,)),
        ],
        compiler_params=pltpu.CompilerParams(vmem_limit_bytes=VMEM_LIMIT),
        cost_estimate=pl.CostEstimate(
            flops=2 * experts * per * width * (7 * ff + 3 * tok),
            bytes_accessed=2 * total * 3 * width + 12 * experts * width * ff,
            transcendentals=experts * per * ff,
        ),
    )(own, *pieces, *weights)


def backward_kernel(cfg, *refs):
    tok, width, ff, experts, cap, sizes, quarters, last = cfg
    refs = list(refs)
    take = lambda k: [refs.pop(0) for _ in range(k)]
    pieces = [take(len(sizes)) for _ in range(quarters)]
    saved = [take(4) for _ in range(quarters)]
    wd, dd = take(2)
    if last:
        in_gu, in_d = take(2)
        gate_hbm, up_hbm, down_hbm = take(3)
    else:
        out_gu, out_d = take(2)
    (rm, sel, grad, hid, rows, wdv, ddv, got, gud, acc_gu, acc_d) = take(11)
    if last:
        gate, up, down = take(3)
    (sems,) = take(1)
    copies = Copies(sems)
    n_blocks = sum(sizes) // tok
    per = n_blocks * cap

    def load(q):
        slot = q % 2
        rows_hbm, sel_hbm, grad_hbm, hid_hbm = saved[q]
        at, started = 0, []
        started.append(copies.start(sel_hbm, sel.at[slot]))
        for size, ref in zip(sizes, pieces[q]):
            started.append(copies.start(ref, rm.at[slot, pl.ds(at, size)]))
            at += size
        started.append(copies.start(grad_hbm, grad.at[slot]))
        for e in range(experts):
            where = pl.ds(q * per, per)
            started.append(copies.start(hid_hbm.at[e], hid.at[e, where]))
            started.append(copies.start(rows_hbm.at[e], rows.at[e, where]))
        return started

    waiting = [load(0)]
    weights = [copies.start(wd, wdv), copies.start(dd, ddv)]
    if last:
        acc_in = [copies.start(in_gu, acc_gu), copies.start(in_d, acc_d)]
    step = 16
    for q in range(quarters):
        slot = q % 2
        if q + 1 < quarters:
            waiting.append(load(q + 1))
        for c in waiting[q]:
            c.wait()
        if q == 0:
            for c in weights:
                c.wait()
        for b in range(n_blocks):
            picked = dot(sel[slot, b], rm[slot, b * tok : (b + 1) * tok, :]).astype(BF16)
            for e in range(experts):
                at = q * per + b * cap
                got[e, at : at + cap, :] = picked[e * cap : (e + 1) * cap]
        for e in range(experts):
            r = got[e, q * per : (q + 1) * per, 0:width]
            m = got[e, q * per : (q + 1) * per, width:]
            grad_h = dot_columns(r, wdv[e])
            grad_d = dot_columns(m, wdv[e]) + dot_columns(r, ddv[e])
            for k in range(0, per, step):
                at = slice(k, k + step)
                to = slice(q * per + k, q * per + k + step)
                gh, gd = grad_h[at], grad_d[at]
                part = lambda i: grad[slot, e, at, i * ff : (i + 1) * ff]
                gud[e, to, 0:ff] = (gd * part(0) + gh * part(1)).astype(BF16)
                gud[e, to, ff:] = (gd * part(2) + gh * part(3)).astype(BF16)

    done = []
    if last:
        for c in acc_in:
            c.wait()
    for e in range(experts):
        gu = dot_rows(rows[e], gud[e])
        if last:
            gu = (gu + acc_gu[e]).astype(BF16)
            gate[e] = gu[:, 0:ff]
            up[e] = gu[:, ff:]
            done.append(copies.start(gate.at[e], gate_hbm.at[e]))
            done.append(copies.start(up.at[e], up_hbm.at[e]))
        else:
            acc_gu[e] = gu
            done.append(copies.start(acc_gu.at[e], out_gu.at[e]))
        d = dot_rows(hid[e, :, ff:], got[e, :, 0:width])
        d += dot_rows(hid[e, :, 0:ff], got[e, :, width:])
        if last:
            down[e] = (d + acc_d[e]).astype(BF16)
            done.append(copies.start(down.at[e], down_hbm.at[e]))
        else:
            acc_d[e] = d
            done.append(copies.start(acc_d.at[e], out_d.at[e]))
    for c in done:
        c.wait()


def backward(quarters, wd, dd, tok, cap, acc=None):
    experts, ff, width = wd.shape
    count = len(quarters)
    last = acc is not None
    sizes = tuple(p.shape[0] for p in quarters[0][0])
    total = sum(sizes)
    n_blocks = total // tok
    per = n_blocks * cap
    shape = jax.ShapeDtypeStruct
    operands = [p for q in quarters for p in q[0]] + [s for q in quarters for s in q[1]] + [wd, dd]
    gu, d = (experts, width, 2 * ff), (experts, ff, width)
    if last:
        operands += list(acc)
        outs = [shape((experts, width, ff), BF16)] * 2 + [shape(d, BF16)]
    else:
        outs = [shape(gu, F32), shape(d, F32)]
    scratch = [
        pltpu.VMEM((2, total, 2 * width), BF16),
        pltpu.VMEM((2, n_blocks, experts * cap, tok), BF16),
        pltpu.VMEM((2, experts, per, 4 * ff), F32),
        pltpu.VMEM((experts, count * per, 2 * ff), BF16),
        pltpu.VMEM((experts, count * per, width), BF16),
        pltpu.VMEM(d, BF16),
        pltpu.VMEM(d, BF16),
        pltpu.VMEM((experts, count * per, 2 * width), BF16),
        pltpu.VMEM((experts, count * per, 2 * ff), BF16),
        pltpu.VMEM(gu, F32),
        pltpu.VMEM(d, F32),
    ]
    if last:
        scratch += [pltpu.VMEM(o.shape, BF16) for o in outs]
    n_sems = count * (len(sizes) + 2 + 2 * experts) + 4 + 3 * experts
    return pl.pallas_call(
        functools.partial(
            backward_kernel, (tok, width, ff, experts, cap, sizes, count, last)
        ),
        in_specs=[ANY] * len(operands),
        out_specs=[ANY] * len(outs),
        out_shape=outs,
        scratch_shapes=scratch + [pltpu.SemaphoreType.DMA((n_sems,))],
        compiler_params=pltpu.CompilerParams(vmem_limit_bytes=VMEM_LIMIT),
        cost_estimate=pl.CostEstimate(
            flops=2 * experts * count * per * width * (7 * ff + 2 * tok),
            bytes_accessed=2 * count * total * 3 * width + 12 * experts * width * ff,
            transcendentals=0,
        ),
    )(*operands)


def local(
    tokens, target, expert_ids, gate_weights, w_gate, w_up, w_down, dir_gate, dir_up, dir_down
):
    n = lax.axis_size("expert")
    me = lax.axis_index("expert")
    nz = n // 4
    experts, width, ff = w_gate.shape
    tok, top_k = expert_ids.shape
    capacity = max(2, 3 * tok * top_k // (2 * experts * n))
    cap = -(-capacity // 16) * 16

    def send(x, to):
        return lax.ppermute(x, "expert", [(i, to(i)) for i in range(n)])

    ahead = lambda x: send(x, lambda i: (i + 4) % n)
    side = lambda x: send(x, lambda i: i ^ 2)
    core = lambda x: send(x, lambda i: i ^ 1)

    def add(a, b):
        return a.astype(F32) + b.astype(F32)

    def gather(x):
        quarters = []
        a = x
        for d in range(nz):
            if d:
                a = ahead(a)
            b = side(a)
            quarters.append((a, b, core(a), core(b)))
        return quarters

    def scatter_sum(parts):
        def plane(near, far):
            got = core(far)
            s = add(near[tok:], got[tok:]).astype(BF16)
            return add(add(near[0:tok], got[0:tok]), side(s))

        total = None
        for d in [*range(1, nz), 0]:
            s = plane(*parts[d])
            total = s if total is None else s + ahead(total.astype(BF16)).astype(F32)
        return total

    exact = lambda a: lax.reduce_precision(a, 8, 7)
    high = exact(gate_weights)
    middle = exact(gate_weights - high)
    low = gate_weights - high - middle
    routes = jnp.concatenate([expert_ids.astype(F32), high, middle, low], 1).astype(BF16)
    routes = jnp.pad(routes, ((0, 0), (0, LANES - 4 * top_k)))
    own = (me * experts).astype(jnp.int32).reshape(1)
    weights = (w_gate, w_up, dir_gate, dir_up, w_down, dir_down)

    x = gather(jnp.concatenate([tokens, routes], 1))
    parts, saved = [], []
    for d in range(nz):
        near, far, *rest = forward(own, x[d], weights, tok, cap, top_k)
        parts.append((near, far))
        saved.append(rest)
    total = scatter_sum(parts)
    total = jnp.concatenate([total[:, 0:width] - target.astype(F32), total[:, width:]], 1)
    rm = gather(total.astype(BF16))
    quarters = list(zip(rm, saved))
    acc = backward(quarters[:-1], w_down, dir_down, tok, cap)
    return tuple(backward(quarters[-1:], w_down, dir_down, tok, cap, acc=acc))


def solution(mesh):
    in_specs = (
        P(("groups", "expert"), None),
        P(("groups", "expert"), None),
        P(("groups", "expert"), None),
        P(("groups", "expert"), None),
        P("expert", None, None),
        P("expert", None, None),
        P("expert", None, None),
        P("expert", None, None),
        P("expert", None, None),
        P("expert", None, None),
    )
    out_specs = (
        P(("groups", "expert"), None, None),
        P(("groups", "expert"), None, None),
        P(("groups", "expert"), None, None),
    )
    return jax.shard_map(local, mesh=mesh, in_specs=in_specs, out_specs=out_specs, check_vma=False)
```

```python
import functools

import jax
import jax.numpy as jnp
from jax import lax
from jax.experimental import pallas as pl
from jax.experimental.pallas import tpu as pltpu
from jax.sharding import PartitionSpec as P

F32 = jnp.float32
BF16 = jnp.bfloat16
VMEM_LIMIT = 56 * 1024 * 1024
LANES = 128
PIN_FA = PIN_FB = True
PIN_C = 3
PIN_Y = 0
RS_ALONG_Z = 0
PIN_M = None
PIN_G = True
PIN_H2 = 0
PIN_H3 = 0
COST = 1000
ANY = pl.BlockSpec(memory_space=pl.ANY)


def dot(a, b):
    return jnp.dot(a, b, preferred_element_type=F32)


def dot_rows(a, b):
    return lax.dot_general(a, b, (((0,), (0,)), ((), ())), preferred_element_type=F32)


def dot_columns(a, b):
    return lax.dot_general(a, b, (((1,), (1,)), ((), ())), preferred_element_type=F32)


class Copies:
    def __init__(self, sems):
        self.sems, self.count = sems, 0

    def start(self, src, dst):
        copy = pltpu.make_async_copy(src, dst, self.sems.at[self.count])
        self.count += 1
        copy.start()
        return copy


def forward_kernel(cfg, own_ref, *refs):
    tok, width, ff, experts, cap, top_k, sizes, quarters = cfg
    refs = list(refs)
    take = lambda k: [refs.pop(0) for _ in range(k)]
    pieces = [take(len(sizes)) for _ in range(quarters)]
    (wg, wu, dg, du, wd, dd) = take(6)
    near_hbm, rows_hbm, sel_hbm, grad_hbm, hid_hbm = [take(quarters) for _ in range(5)]
    far_hbm = [take(4) for _ in range(quarters)]
    (x, w, wdv, ddv, rows, sel, pre, hid, out, part, sems) = take(11)
    copies = Copies(sems)
    quarter = sum(sizes) // tok
    n_blocks = quarters * quarter
    per = n_blocks * cap
    of_quarter = per // quarters
    x_in, at = {}, 0
    for q in range(quarters):
        for size, ref in zip(sizes, pieces[q]):
            x_in[at // tok] = copies.start(ref, x.at[pl.ds(at, size)])
            at += size
    w_in, d_in = [], []
    for e in range(experts):
        w_in.append(
            [
                copies.start(src.at[e], w.at[e, :, pl.ds(k * ff, ff)])
                for k, src in enumerate((wg, wu, dg, du))
            ]
        )
        d_in.append([copies.start(wd.at[e], wdv.at[e]), copies.start(dd.at[e], ddv.at[e])])

    before = lax.broadcasted_iota(jnp.int32, (tok, tok), 0) < lax.broadcasted_iota(
        jnp.int32, (tok, tok), 1
    )
    before = before.astype(BF16)
    place = lax.broadcasted_iota(jnp.int32, (cap, tok), 0).astype(F32)
    weight = [[] for _ in range(experts)]
    for b in range(n_blocks):
        if b in x_in:
            x_in[b].wait()
        xb = x[b * tok : (b + 1) * tok, :]
        routes = xb[:, width : width + LANES].astype(F32).T
        ids = routes[0:top_k]
        gates = (routes[top_k : 2 * top_k] + routes[2 * top_k : 3 * top_k]) + routes[
            3 * top_k : 4 * top_k
        ]
        for e in range(experts):
            named = ids == (own_ref[0] + e).astype(F32)
            hit = jnp.sum(jnp.where(named, 1.0, 0.0), axis=0, keepdims=True)
            gate = jnp.sum(jnp.where(named, gates, 0.0), axis=0, keepdims=True)
            rank = dot(jnp.broadcast_to(hit, (8, tok)).astype(BF16), before)[0:1]
            chosen = jnp.where((rank == place) & (hit > 0.0), 1.0, 0.0)
            weight[e].append(jnp.sum(chosen * gate, axis=1, keepdims=True))
            sel[b, e * cap : (e + 1) * cap, :] = chosen.astype(BF16)
        picked = dot(sel[b], xb[:, 0:width]).astype(BF16)
        for e in range(experts):
            rows[e, b * cap : (b + 1) * cap, :] = picked[e * cap : (e + 1) * cap]
    done = []

    def save(src, dst):
        for q in range(quarters):
            for e in range(experts):
                done.append(
                    copies.start(src.at[e, pl.ds(q * of_quarter, of_quarter)], dst[q].at[e])
                )

    for q in range(quarters):
        done.append(copies.start(sel.at[pl.ds(q * quarter, quarter)], sel_hbm[q]))
    save(rows, rows_hbm)

    step = 16
    for e in range(experts):
        for c in w_in[e]:
            c.wait()
        pre[e] = dot(rows[e], w[e])
    for e in range(experts):
        g_all = jnp.concatenate(weight[e], axis=0)
        for r in range(0, per, step):
            at = slice(r, r + step)
            g = g_all[at]
            p, u = pre[e, at, 0:ff], pre[e, at, ff : 2 * ff]
            dgv, duv = pre[e, at, 2 * ff : 3 * ff], pre[e, at, 3 * ff :]
            s = jax.nn.sigmoid(p)
            act = g * (p * s)
            slope = g * (s * (1.0 + p * (1.0 - s)))
            curv = g * (s * (1.0 - s) * (2.0 + p * (1.0 - 2.0 * s)))
            slope_up = slope * u
            hid[e, at, 0:ff] = (act * u).astype(BF16)
            hid[e, at, ff:] = (slope_up * dgv + act * duv).astype(BF16)
            pre[e, at, 0:ff] = slope_up
            pre[e, at, ff : 2 * ff] = curv * dgv * u + slope * duv
            pre[e, at, 2 * ff : 3 * ff] = act
            pre[e, at, 3 * ff :] = slope * dgv
        for c in d_in[e]:
            c.wait()
        h, hd = hid[e, :, 0:ff], hid[e, :, ff:]
        o = dot(h, wdv[e]).astype(BF16)
        od = (dot(hd, wdv[e]) + dot(h, ddv[e])).astype(BF16)
        for b in range(n_blocks):
            out[b, e * cap : (e + 1) * cap, 0:width] = o[b * cap : (b + 1) * cap]
            out[b, e * cap : (e + 1) * cap, width:] = od[b * cap : (b + 1) * cap]
    half = quarter // 2
    for q in reversed(range(quarters)):
        for near in (False, True):
            first = q * quarter + (0 if near else half)
            for b in range(first, first + half):
                part[b * tok : (b + 1) * tok, :] = dot_rows(sel[b], out[b]).astype(BF16)
            if near:
                done.append(copies.start(part.at[pl.ds(first * tok, half * tok)], near_hbm[q]))
                continue
            for y in reversed(range(half)):
                for k in range(2):
                    sent = part.at[pl.ds((first + y) * tok, tok), pl.ds(k * width, width)]
                    done.append(copies.start(sent, far_hbm[q][2 * y + k]))
    save(pre, grad_hbm)
    save(hid, hid_hbm)
    for c in done:
        c.wait()


def forward(own, quarters, weights, tok, cap, top_k):
    wg, wd = weights[0], weights[4]
    experts, width, ff = wg.shape
    count = len(quarters)
    sizes = tuple(p.shape[0] for p in quarters[0])
    total = sum(sizes)
    n_blocks = total // tok
    per = n_blocks * cap
    shape = jax.ShapeDtypeStruct
    outs = (
        [shape((total // 2, 2 * width), BF16)] * count
        + [shape((experts, per, width), BF16)] * count
        + [shape((n_blocks, experts * cap, tok), BF16)] * count
        + [shape((experts, per, 4 * ff), F32)] * count
        + [shape((experts, per, 2 * ff), BF16)] * count
        + [shape((tok, width), BF16)] * (4 * count)
    )
    operands = [p for q in quarters for p in q] + list(weights)
    rows = count * per
    n_sems = count * (len(sizes) + 6 + 3 * experts) + 6 * experts
    flat = pl.pallas_call(
        functools.partial(
            forward_kernel, (tok, width, ff, experts, cap, top_k, sizes, count)
        ),
        in_specs=[pl.BlockSpec(memory_space=pltpu.SMEM)] + [ANY] * len(operands),
        out_specs=[ANY] * len(outs),
        out_shape=outs,
        scratch_shapes=[
            pltpu.VMEM((count * total, quarters[0][0].shape[1]), BF16),
            pltpu.VMEM((experts, width, 4 * ff), BF16),
            pltpu.VMEM((experts, ff, width), BF16),
            pltpu.VMEM((experts, ff, width), BF16),
            pltpu.VMEM((experts, rows, width), BF16),
            pltpu.VMEM((count * n_blocks, experts * cap, tok), BF16),
            pltpu.VMEM((experts, rows, 4 * ff), F32),
            pltpu.VMEM((experts, rows, 2 * ff), BF16),
            pltpu.VMEM((count * n_blocks, experts * cap, 2 * width), BF16),
            pltpu.VMEM((count * total, 2 * width), BF16),
            pltpu.SemaphoreType.DMA((n_sems,)),
        ],
        compiler_params=pltpu.CompilerParams(vmem_limit_bytes=VMEM_LIMIT),
        cost_estimate=pl.CostEstimate(
            flops=COST * 2 * experts * rows * width * (7 * ff + 3 * tok) // 100,
            bytes_accessed=COST
            * (2 * count * total * 3 * width + 12 * experts * width * ff)
            // 100,
            transcendentals=0,
        ),
    )(own, *operands)
    far = flat[5 * count :]
    return [[*flat[q : 5 * count : count], far[4 * q : 4 * q + 4]] for q in range(count)]


def grad_kernel(cfg, *refs):
    tok, width, ff, experts, cap, sizes, earlier, last = cfg
    refs = list(refs)
    take = lambda k: [refs.pop(0) for _ in range(k)]
    pieces = [take(len(sizes)) for _ in range(2)]
    sel_hbm, grad_hbm, wd, dd = take(4)
    n_blocks = sum(sizes) // tok
    per = n_blocks * cap
    base = earlier * per
    if last:
        rows_hbm, hid_hbm = take(earlier + 1), take(earlier + 1)
        got_hbm, gud_hbm = take(earlier), take(earlier)
        gate_hbm, up_hbm, down_hbm = take(3)
        rm, sel, grad, wdv, ddv, got, gud, rows, hid, gate, up, down, sems = take(13)
    else:
        got_out, gud_out = take(2)
        rm, sel, grad, wdv, ddv, got, gud, sems = take(8)
    copies = Copies(sems)

    loads = []
    at = 0
    for i, size in enumerate(sizes):
        loads.append([copies.start(p[i], rm.at[k, pl.ds(at, size)]) for k, p in enumerate(pieces)])
        at += size
    first = copies.start(sel_hbm, sel)
    weights = [copies.start(wd, wdv), copies.start(dd, ddv), copies.start(grad_hbm, grad)]
    late = []
    if last:
        for q in range(earlier + 1):
            at = pl.ds(q * per, per)
            for e in range(experts):
                late.append(copies.start(rows_hbm[q].at[e], rows.at[e, at]))
                late.append(copies.start(hid_hbm[q].at[e], hid.at[e, at]))
                if q < earlier:
                    late.append(copies.start(gud_hbm[q].at[e], gud.at[e, at]))
                    for k in range(2):
                        late.append(copies.start(got_hbm[q].at[k, e], got.at[k, e, at]))
    first.wait()
    at = 0
    for i, size in enumerate(sizes):
        for c in loads[i]:
            c.wait()
        for b in range(at // tok, (at + size) // tok):
            for k in range(2):
                picked = dot(sel[b], rm[k, b * tok : (b + 1) * tok, :]).astype(BF16)
                for e in range(experts):
                    to = base + b * cap
                    got[k, e, to : to + cap, :] = picked[e * cap : (e + 1) * cap]
        at += size
    for c in weights:
        c.wait()
    done = []
    if not last:
        done.append(copies.start(got, got_out))
    step = 16
    for e in range(experts):
        r, m = got[0, e, base : base + per, :], got[1, e, base : base + per, :]
        grad_h = dot_columns(r, wdv[e])
        grad_d = dot_columns(m, wdv[e]) + dot_columns(r, ddv[e])
        for k in range(0, per, step):
            at, to = slice(k, k + step), slice(base + k, base + k + step)
            gh, gd = grad_h[at], grad_d[at]
            part = lambda i: grad[e, at, i * ff : (i + 1) * ff]
            gud[e, to, 0:ff] = (gd * part(0) + gh * part(1)).astype(BF16)
            gud[e, to, ff:] = (gd * part(2) + gh * part(3)).astype(BF16)
    if not last:
        done.append(copies.start(gud, gud_out))
    else:
        for c in late:
            c.wait()
        for e in range(experts):
            d = dot_rows(hid[e, :, ff:], got[0, e]) + dot_rows(hid[e, :, 0:ff], got[1, e])
            down[e] = d.astype(BF16)
            done.append(copies.start(down.at[e], down_hbm.at[e]))
            gu = dot_rows(rows[e], gud[e]).astype(BF16)
            gate[e] = gu[:, 0:ff]
            up[e] = gu[:, ff:]
            done.append(copies.start(gate.at[e], gate_hbm.at[e]))
            done.append(copies.start(up.at[e], up_hbm.at[e]))
    for c in done:
        c.wait()


def backward(r_pieces, m_pieces, saved, wd, dd, tok, cap, before=()):
    experts, ff, width = wd.shape
    last = len(before) > 0
    earlier = len(before)
    sizes = tuple(p.shape[0] for p in r_pieces)
    total = sum(sizes)
    n_blocks = total // tok
    per = n_blocks * cap
    count = (earlier + 1) * per
    shape = jax.ShapeDtypeStruct
    d = (experts, ff, width)
    _, sel, grad, _ = saved[-1]
    operands = [*r_pieces, *m_pieces, sel, grad, wd, dd]
    scratch = [
        pltpu.VMEM((2, total, width), BF16),
        pltpu.VMEM((n_blocks, experts * cap, tok), BF16),
        pltpu.VMEM((experts, per, 4 * ff), F32),
        pltpu.VMEM(d, BF16),
        pltpu.VMEM(d, BF16),
        pltpu.VMEM((2, experts, count, width), BF16),
        pltpu.VMEM((experts, count, 2 * ff), BF16),
    ]
    n_sems = 2 * len(sizes) + 4
    if last:
        operands += [s[0] for s in saved] + [s[3] for s in saved]
        operands += [b[0] for b in before] + [b[1] for b in before]
        outs = [shape((experts, width, ff), BF16)] * 2 + [shape(d, BF16)]
        scratch += [pltpu.VMEM((experts, count, width), BF16), pltpu.VMEM((experts, count, 2 * ff), BF16)]
        scratch += [pltpu.VMEM(o.shape, BF16) for o in outs]
        n_sems += experts * (2 + 5 * earlier) + 3 * experts
        macs = experts * count * width * 4 * ff
    else:
        outs = [
            shape((2, experts, per, width), BF16),
            shape((experts, per, 2 * ff), BF16),
        ]
        n_sems += 2
        macs = 0
    return pl.pallas_call(
        functools.partial(
            grad_kernel, (tok, width, ff, experts, cap, sizes, earlier, last)
        ),
        in_specs=[ANY] * len(operands),
        out_specs=[ANY] * len(outs),
        out_shape=outs,
        scratch_shapes=scratch + [pltpu.SemaphoreType.DMA((n_sems,))],
        compiler_params=pltpu.CompilerParams(vmem_limit_bytes=VMEM_LIMIT),
        cost_estimate=pl.CostEstimate(
            flops=COST * 2 * (experts * per * width * (3 * ff + 2 * tok) + macs) // 100,
            bytes_accessed=COST * (2 * total * 3 * width + 4 * experts * width * ff) // 100,
            transcendentals=0,
        ),
    )(*operands)


def local(
    tokens, target, expert_ids, gate_weights, w_gate, w_up, w_down, dir_gate, dir_up, dir_down
):
    n = lax.axis_size("expert")
    me = lax.axis_index("expert")
    nz = n // 4
    experts, width, ff = w_gate.shape
    tok, top_k = expert_ids.shape
    capacity = max(2, 3 * tok * top_k // (2 * experts * n))
    cap = -(-capacity // 16) * 16

    def send(x, to):
        return lax.ppermute(x, "expert", [(i, to(i)) for i in range(n)])

    ahead = lambda x: send(x, lambda i: (i + 4) % n)
    side = lambda x: send(x, lambda i: i ^ 2)
    core = lambda x: send(x, lambda i: i ^ 1)

    def add(a, b):
        return a.astype(F32) + b.astype(F32)

    def after(x, *others):
        return lax.optimization_barrier((x, *others))[0]

    def gather(x):
        steps = []
        for d in range(nz):
            if d:
                x = ahead(x)
            steps.append((x, side(x)))
        return steps

    exact = lambda a: lax.reduce_precision(a, 8, 7)
    high = exact(gate_weights)
    middle = exact(gate_weights - high)
    low = gate_weights - high - middle
    routes = jnp.concatenate([expert_ids.astype(F32), high, middle, low], 1).astype(BF16)
    routes = jnp.pad(routes, ((0, 0), (0, LANES - 4 * top_k)))
    own = (me * experts).astype(jnp.int32).reshape(1)
    weights = (w_gate, w_up, dir_gate, dir_up, w_down, dir_down)

    cols = (slice(0, width), slice(width, 2 * width))
    steps = gather(jnp.concatenate([tokens, routes], 1))
    half = nz // 2
    saved = []
    mine, other, over = ([], []), ([], []), ([], [])
    for first, last in ((0, half), (half, nz)):
        start = own
        if first == 0 and PIN_FA:
            start = after(own, steps[min(half, nz - 1)][0])
        if first and PIN_FB:
            start = after(own, *[other[0][1]])
        quarters = [(a, b, core(a), core(b)) for a, b in steps[first:last]]
        for d, (near, *rest, far) in enumerate(
            forward(start, quarters, weights, tok, cap, top_k), first
        ):
            saved.append(rest)
            for k, c in enumerate(cols):
                f = far[2 + k]
                if first and PIN_C >> k & 1:
                    f = after(f, over[k][0 if over[k][1] is None else 1])
                o = add(near[tok:, c], core(f)).astype(BF16)
                if first and PIN_Y >> k & 1:
                    o = after(o, over[k][0])
                if RS_ALONG_Z >> k & 1 and d == 2:
                    o = add(o, ahead(other[k][1])).astype(BF16)
                other[k].append(o)
                over[k].append(None if RS_ALONG_Z >> k & 1 and d == 1 else side(o))
            for k, c in enumerate(cols):
                mine[k].append(add(near[0:tok, c], core(far[k])))

    def ring_sum(k, then=None):
        total = None
        for d in [*range(1, nz), 0]:
            s = mine[k][d] if over[k][d] is None else add(mine[k][d], over[k][d])
            if total is not None:
                t = total.astype(BF16)
                if d == 2 and PIN_H2 >> k & 1:
                    t = after(t, over[k][nz - 1])
                if d == 0 and PIN_H3 >> k & 1:
                    t = after(t, over[k][0])
                if d == 0 and then is not None:
                    t = after(t, then)
                s = s + ahead(t).astype(F32)
            total = s
        return total

    r = gather((ring_sum(0) - target.astype(F32)).astype(BF16))
    ma = ring_sum(1, r[PIN_M[0]][PIN_M[1]] if PIN_M else r[0][0]).astype(BF16)
    mb = side(ma)
    before, nexts = [], [ahead(ma)]
    for d in range(nz):
        (ra, rb) = r[d]
        last_b = after(mb, before[-1][1]) if PIN_G and d == nz - 1 else mb
        pieces = (ra, rb, core(ra), core(rb)), (ma, mb, core(ma), core(last_b))
        if d == nz - 1:
            break
        if PIN_G:
            pieces = ((after(ra, nexts[d]), *pieces[0][1:]), pieces[1])
        before.append(backward(*pieces, saved[d : d + 1], w_down, dir_down, tok, cap))
        ma = nexts[d]
        if PIN_G and d + 2 < nz:
            nexts.append(ahead(ma))
            nexts[d + 1] = after(nexts[d + 1], before[d][1])
        elif d + 2 < nz:
            nexts.append(ahead(ma))
        mb = side(ma)
    return tuple(backward(*pieces, saved, w_down, dir_down, tok, cap, before=before))


def solution(mesh):
    in_specs = (
        P(("groups", "expert"), None),
        P(("groups", "expert"), None),
        P(("groups", "expert"), None),
        P(("groups", "expert"), None),
        P("expert", None, None),
        P("expert", None, None),
        P("expert", None, None),
        P("expert", None, None),
        P("expert", None, None),
        P("expert", None, None),
    )
    out_specs = (
        P(("groups", "expert"), None, None),
        P(("groups", "expert"), None, None),
        P(("groups", "expert"), None, None),
    )
    return jax.shard_map(local, mesh=mesh, in_specs=in_specs, out_specs=out_specs, check_vma=False)
```

```python
import functools

import jax
import jax.numpy as jnp
from jax import lax
from jax.experimental import pallas as pl
from jax.experimental.pallas import tpu as pltpu
from jax.sharding import PartitionSpec as P

F32 = jnp.float32
BF16 = jnp.bfloat16
VMEM_LIMIT = 56 * 1024 * 1024
LANES = 128
PIN_0 = 0
PIN_M = None
PIN_G = True
PIN_H2 = 0
PIN_H3 = 0
COST = 1000
ANY = pl.BlockSpec(memory_space=pl.ANY)


def dot(a, b):
    return jnp.dot(a, b, preferred_element_type=F32)


def dot_rows(a, b):
    return lax.dot_general(a, b, (((0,), (0,)), ((), ())), preferred_element_type=F32)


def dot_columns(a, b):
    return lax.dot_general(a, b, (((1,), (1,)), ((), ())), preferred_element_type=F32)


class Copies:
    def __init__(self, sems):
        self.sems, self.count = sems, 0

    def start(self, src, dst):
        copy = pltpu.make_async_copy(src, dst, self.sems.at[self.count])
        self.count += 1
        copy.start()
        return copy


def forward_kernel(cfg, own_ref, *refs):
    tok, width, ff, experts, cap, top_k, sizes, quarters = cfg
    refs = list(refs)
    take = lambda k: [refs.pop(0) for _ in range(k)]
    pieces = [take(len(sizes)) for _ in range(quarters)]
    (wg, wu, dg, du, wd, dd) = take(6)
    near_hbm, rows_hbm, sel_hbm, grad_hbm, hid_hbm = [take(quarters) for _ in range(5)]
    far_hbm = [take(4) for _ in range(quarters)]
    (x, w, wdv, ddv, rows, sel, pre, hid, out, part, sems) = take(11)
    copies = Copies(sems)
    quarter = sum(sizes) // tok
    n_blocks = quarters * quarter
    per = n_blocks * cap
    of_quarter = per // quarters
    x_in, at = {}, 0
    for q in range(quarters):
        for size, ref in zip(sizes, pieces[q]):
            x_in[at // tok] = copies.start(ref, x.at[pl.ds(at, size)])
            at += size
    w_in, d_in = [], []
    for e in range(experts):
        w_in.append(
            [
                copies.start(src.at[e], w.at[e, :, pl.ds(k * ff, ff)])
                for k, src in enumerate((wg, wu, dg, du))
            ]
        )
        d_in.append([copies.start(wd.at[e], wdv.at[e]), copies.start(dd.at[e], ddv.at[e])])

    before = lax.broadcasted_iota(jnp.int32, (tok, tok), 0) < lax.broadcasted_iota(
        jnp.int32, (tok, tok), 1
    )
    before = before.astype(BF16)
    place = lax.broadcasted_iota(jnp.int32, (cap, tok), 0).astype(F32)
    weight = [[] for _ in range(experts)]
    hits, gates_of = [], []
    for b in range(n_blocks):
        if b in x_in:
            x_in[b].wait()
        routes = x[b * tok : (b + 1) * tok, width : width + LANES].astype(F32).T
        ids = routes[0:top_k]
        gates = (routes[top_k : 2 * top_k] + routes[2 * top_k : 3 * top_k]) + routes[
            3 * top_k : 4 * top_k
        ]
        for e in range(experts):
            named = ids == (own_ref[0] + e).astype(F32)
            hits.append(jnp.sum(jnp.where(named, 1.0, 0.0), axis=0, keepdims=True))
            gates_of.append(jnp.sum(jnp.where(named, gates, 0.0), axis=0, keepdims=True))
    ranks = dot(jnp.concatenate(hits, axis=0).astype(BF16), before)
    for b in range(n_blocks):
        xb = x[b * tok : (b + 1) * tok, :]
        for e in range(experts):
            i = b * experts + e
            chosen = jnp.where((ranks[i : i + 1] == place) & (hits[i] > 0.0), 1.0, 0.0)
            weight[e].append(jnp.sum(chosen * gates_of[i], axis=1, keepdims=True))
            sel[b, e * cap : (e + 1) * cap, :] = chosen.astype(BF16)
        picked = dot(sel[b], xb[:, 0:width]).astype(BF16)
        for e in range(experts):
            rows[e, b * cap : (b + 1) * cap, :] = picked[e * cap : (e + 1) * cap]
    done = []

    def save(src, dst, e):
        for q in range(quarters):
            done.append(
                copies.start(src.at[e, pl.ds(q * of_quarter, of_quarter)], dst[q].at[e])
            )

    for q in range(quarters):
        done.append(copies.start(sel.at[pl.ds(q * quarter, quarter)], sel_hbm[q]))
    for e in range(experts):
        save(rows, rows_hbm, e)

    step = 16
    for e in range(experts):
        for c in w_in[e]:
            c.wait()
        pre[e] = dot(rows[e], w[e])
    for e in range(experts):
        g_all = jnp.concatenate(weight[e], axis=0)
        for r in range(0, per, step):
            at = slice(r, r + step)
            g = g_all[at]
            p, u = pre[e, at, 0:ff], pre[e, at, ff : 2 * ff]
            dgv, duv = pre[e, at, 2 * ff : 3 * ff], pre[e, at, 3 * ff :]
            s = jax.nn.sigmoid(p)
            act = g * (p * s)
            slope = g * (s * (1.0 + p * (1.0 - s)))
            curv = g * (s * (1.0 - s) * (2.0 + p * (1.0 - 2.0 * s)))
            slope_up = slope * u
            hid[e, at, 0:ff] = (act * u).astype(BF16)
            hid[e, at, ff:] = (slope_up * dgv + act * duv).astype(BF16)
            pre[e, at, 0:ff] = slope_up
            pre[e, at, ff : 2 * ff] = curv * dgv * u + slope * duv
            pre[e, at, 2 * ff : 3 * ff] = act
            pre[e, at, 3 * ff :] = slope * dgv
        save(hid, hid_hbm, e)
        save(pre, grad_hbm, e)
        for c in d_in[e]:
            c.wait()
        h, hd = hid[e, :, 0:ff], hid[e, :, ff:]
        o = dot(h, wdv[e]).astype(BF16)
        od = (dot(hd, wdv[e]) + dot(h, ddv[e])).astype(BF16)
        for b in range(n_blocks):
            out[b, e * cap : (e + 1) * cap, 0:width] = o[b * cap : (b + 1) * cap]
            out[b, e * cap : (e + 1) * cap, width:] = od[b * cap : (b + 1) * cap]
    half = quarter // 2
    for q in reversed(range(quarters)):
        for near in (False, True):
            first = q * quarter + (0 if near else half)
            for b in range(first, first + half):
                part[b * tok : (b + 1) * tok, :] = dot_rows(sel[b], out[b]).astype(BF16)
            if near:
                done.append(copies.start(part.at[pl.ds(first * tok, half * tok)], near_hbm[q]))
                continue
            for y in reversed(range(half)):
                for k in range(2):
                    sent = part.at[pl.ds((first + y) * tok, tok), pl.ds(k * width, width)]
                    done.append(copies.start(sent, far_hbm[q][2 * y + k]))
    for c in done:
        c.wait()


def forward(own, quarters, weights, tok, cap, top_k):
    wg, wd = weights[0], weights[4]
    experts, width, ff = wg.shape
    count = len(quarters)
    sizes = tuple(p.shape[0] for p in quarters[0])
    total = sum(sizes)
    n_blocks = total // tok
    per = n_blocks * cap
    shape = jax.ShapeDtypeStruct
    outs = (
        [shape((total // 2, 2 * width), BF16)] * count
        + [shape((experts, per, width), BF16)] * count
        + [shape((n_blocks, experts * cap, tok), BF16)] * count
        + [shape((experts, per, 4 * ff), F32)] * count
        + [shape((experts, per, 2 * ff), BF16)] * count
        + [shape((tok, width), BF16)] * (4 * count)
    )
    operands = [p for q in quarters for p in q] + list(weights)
    rows = count * per
    n_sems = count * (len(sizes) + 6 + 3 * experts) + 6 * experts
    flat = pl.pallas_call(
        functools.partial(
            forward_kernel, (tok, width, ff, experts, cap, top_k, sizes, count)
        ),
        in_specs=[pl.BlockSpec(memory_space=pltpu.SMEM)] + [ANY] * len(operands),
        out_specs=[ANY] * len(outs),
        out_shape=outs,
        scratch_shapes=[
            pltpu.VMEM((count * total, quarters[0][0].shape[1]), BF16),
            pltpu.VMEM((experts, width, 4 * ff), BF16),
            pltpu.VMEM((experts, ff, width), BF16),
            pltpu.VMEM((experts, ff, width), BF16),
            pltpu.VMEM((experts, rows, width), BF16),
            pltpu.VMEM((count * n_blocks, experts * cap, tok), BF16),
            pltpu.VMEM((experts, rows, 4 * ff), F32),
            pltpu.VMEM((experts, rows, 2 * ff), BF16),
            pltpu.VMEM((count * n_blocks, experts * cap, 2 * width), BF16),
            pltpu.VMEM((count * total, 2 * width), BF16),
            pltpu.SemaphoreType.DMA((n_sems,)),
        ],
        compiler_params=pltpu.CompilerParams(vmem_limit_bytes=VMEM_LIMIT),
        cost_estimate=pl.CostEstimate(
            flops=COST * 2 * experts * rows * width * (7 * ff + 3 * tok) // 100,
            bytes_accessed=COST
            * (2 * count * total * 3 * width + 12 * experts * width * ff)
            // 100,
            transcendentals=0,
        ),
    )(own, *operands)
    far = flat[5 * count :]
    return [[*flat[q : 5 * count : count], far[4 * q : 4 * q + 4]] for q in range(count)]


def grad_kernel(cfg, *refs):
    tok, width, ff, experts, cap, sizes, earlier, last = cfg
    refs = list(refs)
    take = lambda k: [refs.pop(0) for _ in range(k)]
    pieces = [take(len(sizes)) for _ in range(2)]
    sel_hbm, grad_hbm, wd, dd = take(4)
    n_blocks = sum(sizes) // tok
    per = n_blocks * cap
    base = earlier * per
    if last:
        rows_hbm, hid_hbm = take(earlier + 1), take(earlier + 1)
        got_hbm, gud_hbm = take(earlier), take(earlier)
        gate_hbm, up_hbm, down_hbm = take(3)
        rm, sel, grad, wdv, ddv, got, gud, rows, hid, gate, up, down, sems = take(13)
    else:
        got_out, gud_out = take(2)
        rm, sel, grad, wdv, ddv, got, gud, sems = take(8)
    copies = Copies(sems)

    loads = []
    at = 0
    for i, size in enumerate(sizes):
        loads.append([copies.start(p[i], rm.at[k, pl.ds(at, size)]) for k, p in enumerate(pieces)])
        at += size
    first = copies.start(sel_hbm, sel)
    weights = [copies.start(wd, wdv), copies.start(dd, ddv), copies.start(grad_hbm, grad)]
    late = []
    if last:
        for q in range(earlier + 1):
            at = pl.ds(q * per, per)
            for e in range(experts):
                late.append(copies.start(rows_hbm[q].at[e], rows.at[e, at]))
                late.append(copies.start(hid_hbm[q].at[e], hid.at[e, at]))
                if q < earlier:
                    late.append(copies.start(gud_hbm[q].at[e], gud.at[e, at]))
                    for k in range(2):
                        late.append(copies.start(got_hbm[q].at[k, e], got.at[k, e, at]))
    first.wait()
    at = 0
    for i, size in enumerate(sizes):
        for c in loads[i]:
            c.wait()
        for b in range(at // tok, (at + size) // tok):
            for k in range(2):
                picked = dot(sel[b], rm[k, b * tok : (b + 1) * tok, :]).astype(BF16)
                for e in range(experts):
                    to = base + b * cap
                    got[k, e, to : to + cap, :] = picked[e * cap : (e + 1) * cap]
        at += size
    for c in weights:
        c.wait()
    done = []
    if not last:
        done.append(copies.start(got, got_out))
    step = 16
    for e in range(experts):
        r, m = got[0, e, base : base + per, :], got[1, e, base : base + per, :]
        grad_h = dot_columns(r, wdv[e])
        grad_d = dot_columns(m, wdv[e]) + dot_columns(r, ddv[e])
        for k in range(0, per, step):
            at, to = slice(k, k + step), slice(base + k, base + k + step)
            gh, gd = grad_h[at], grad_d[at]
            part = lambda i: grad[e, at, i * ff : (i + 1) * ff]
            gud[e, to, 0:ff] = (gd * part(0) + gh * part(1)).astype(BF16)
            gud[e, to, ff:] = (gd * part(2) + gh * part(3)).astype(BF16)
    if not last:
        done.append(copies.start(gud, gud_out))
    else:
        for c in late:
            c.wait()
        for e in range(experts):
            d = dot_rows(hid[e, :, ff:], got[0, e]) + dot_rows(hid[e, :, 0:ff], got[1, e])
            down[e] = d.astype(BF16)
            done.append(copies.start(down.at[e], down_hbm.at[e]))
            gu = dot_rows(rows[e], gud[e]).astype(BF16)
            gate[e] = gu[:, 0:ff]
            up[e] = gu[:, ff:]
            done.append(copies.start(gate.at[e], gate_hbm.at[e]))
            done.append(copies.start(up.at[e], up_hbm.at[e]))
    for c in done:
        c.wait()


def backward(r_pieces, m_pieces, saved, wd, dd, tok, cap, before=()):
    experts, ff, width = wd.shape
    last = len(before) > 0
    earlier = len(before)
    sizes = tuple(p.shape[0] for p in r_pieces)
    total = sum(sizes)
    n_blocks = total // tok
    per = n_blocks * cap
    count = (earlier + 1) * per
    shape = jax.ShapeDtypeStruct
    d = (experts, ff, width)
    _, sel, grad, _ = saved[-1]
    operands = [*r_pieces, *m_pieces, sel, grad, wd, dd]
    scratch = [
        pltpu.VMEM((2, total, width), BF16),
        pltpu.VMEM((n_blocks, experts * cap, tok), BF16),
        pltpu.VMEM((experts, per, 4 * ff), F32),
        pltpu.VMEM(d, BF16),
        pltpu.VMEM(d, BF16),
        pltpu.VMEM((2, experts, count, width), BF16),
        pltpu.VMEM((experts, count, 2 * ff), BF16),
    ]
    n_sems = 2 * len(sizes) + 4
    if last:
        operands += [s[0] for s in saved] + [s[3] for s in saved]
        operands += [b[0] for b in before] + [b[1] for b in before]
        outs = [shape((experts, width, ff), BF16)] * 2 + [shape(d, BF16)]
        scratch += [pltpu.VMEM((experts, count, width), BF16), pltpu.VMEM((experts, count, 2 * ff), BF16)]
        scratch += [pltpu.VMEM(o.shape, BF16) for o in outs]
        n_sems += experts * (2 + 5 * earlier) + 3 * experts
        macs = experts * count * width * 4 * ff
    else:
        outs = [
            shape((2, experts, per, width), BF16),
            shape((experts, per, 2 * ff), BF16),
        ]
        n_sems += 2
        macs = 0
    return pl.pallas_call(
        functools.partial(
            grad_kernel, (tok, width, ff, experts, cap, sizes, earlier, last)
        ),
        in_specs=[ANY] * len(operands),
        out_specs=[ANY] * len(outs),
        out_shape=outs,
        scratch_shapes=scratch + [pltpu.SemaphoreType.DMA((n_sems,))],
        compiler_params=pltpu.CompilerParams(vmem_limit_bytes=VMEM_LIMIT),
        cost_estimate=pl.CostEstimate(
            flops=COST * 2 * (experts * per * width * (3 * ff + 2 * tok) + macs) // 100,
            bytes_accessed=COST * (2 * total * 3 * width + 4 * experts * width * ff) // 100,
            transcendentals=0,
        ),
    )(*operands)


def local(
    tokens, target, expert_ids, gate_weights, w_gate, w_up, w_down, dir_gate, dir_up, dir_down
):
    n = lax.axis_size("expert")
    me = lax.axis_index("expert")
    nz = n // 4
    experts, width, ff = w_gate.shape
    tok, top_k = expert_ids.shape
    capacity = max(2, 3 * tok * top_k // (2 * experts * n))
    cap = -(-capacity // 16) * 16

    def send(x, to):
        return lax.ppermute(x, "expert", [(i, to(i)) for i in range(n)])

    ahead = lambda x: send(x, lambda i: (i + 4) % n)
    side = lambda x: send(x, lambda i: i ^ 2)
    core = lambda x: send(x, lambda i: i ^ 1)

    def add(a, b):
        return a.astype(F32) + b.astype(F32)

    def after(x, *others):
        return lax.optimization_barrier((x, *others))[0]

    def gather(x):
        steps = []
        for d in range(nz):
            if d:
                x = ahead(x)
            steps.append((x, side(x)))
        return steps

    exact = lambda a: lax.reduce_precision(a, 8, 7)
    high = exact(gate_weights)
    middle = exact(gate_weights - high)
    low = gate_weights - high - middle
    routes = jnp.concatenate([expert_ids.astype(F32), high, middle, low], 1).astype(BF16)
    routes = jnp.pad(routes, ((0, 0), (0, LANES - 4 * top_k)))
    own = (me * experts).astype(jnp.int32).reshape(1)
    weights = (w_gate, w_up, dir_gate, dir_up, w_down, dir_down)

    cols = (slice(0, width), slice(width, 2 * width))
    half = nz // 2
    saved = []
    mine, other, over = ([], []), ([], []), ([], [])
    a = jnp.concatenate([tokens, routes], 1)
    ring = [a]
    for d in range(1, nz):
        ring.append(ahead(ring[-1]))
    sides = [side(a) for a in ring[: half + 1]]
    for first, last in ((0, half), (half, nz)):
        start = own
        if first == 0:
            start = after(own, ring[min(half, nz - 1)])
        else:
            start = after(own, other[0][1])
            for d in range(half + 1, nz):
                sides.append(side(after(ring[d], saved[0][1], sides[half])))
        quarters = [(ring[d], sides[d], core(ring[d]), core(sides[d])) for d in range(first, last)]
        for d, (near, *rest, far) in enumerate(
            forward(start, quarters, weights, tok, cap, top_k), first
        ):
            saved.append(rest)
            for k, c in enumerate(cols):
                f = far[2 + k]
                if first:
                    f = after(f, over[k][1], *(over[j][0] for j in range(2) if PIN_0 >> j & 1))
                o = add(near[tok:, c], core(f)).astype(BF16)
                other[k].append(o)
                over[k].append(side(o))
            for k, c in enumerate(cols):
                mine[k].append(add(near[0:tok, c], core(far[k])))

    def ring_sum(k, then=None):
        total = None
        for d in [*range(1, nz), 0]:
            s = add(mine[k][d], over[k][d])
            if total is not None:
                t = total.astype(BF16)
                if d == 2 and PIN_H2 >> k & 1:
                    t = after(t, over[k][nz - 1])
                if d == 0 and PIN_H3 >> k & 1:
                    t = after(t, over[k][0])
                if d == 0 and then is not None:
                    t = after(t, then)
                s = s + ahead(t).astype(F32)
            total = s
        return total

    r = gather((ring_sum(0) - target.astype(F32)).astype(BF16))
    ma = ring_sum(1, r[PIN_M[0]][PIN_M[1]] if PIN_M else r[0][0]).astype(BF16)
    mb = side(ma)
    before, nexts = [], [ahead(ma)]
    for d in range(nz):
        (ra, rb) = r[d]
        last_b = after(mb, before[-1][1]) if PIN_G and d == nz - 1 else mb
        pieces = (ra, rb, core(ra), core(rb)), (ma, mb, core(ma), core(last_b))
        if d == nz - 1:
            break
        if PIN_G:
            pieces = ((after(ra, nexts[d]), *pieces[0][1:]), pieces[1])
        before.append(backward(*pieces, saved[d : d + 1], w_down, dir_down, tok, cap))
        ma = nexts[d]
        if PIN_G and d + 2 < nz:
            nexts.append(ahead(ma))
            nexts[d + 1] = after(nexts[d + 1], before[d][1])
        elif d + 2 < nz:
            nexts.append(ahead(ma))
        mb = side(ma)
    return tuple(backward(*pieces, saved, w_down, dir_down, tok, cap, before=before))


def solution(mesh):
    in_specs = (
        P(("groups", "expert"), None),
        P(("groups", "expert"), None),
        P(("groups", "expert"), None),
        P(("groups", "expert"), None),
        P("expert", None, None),
        P("expert", None, None),
        P("expert", None, None),
        P("expert", None, None),
        P("expert", None, None),
        P("expert", None, None),
    )
    out_specs = (
        P(("groups", "expert"), None, None),
        P(("groups", "expert"), None, None),
        P(("groups", "expert"), None, None),
    )
    return jax.shard_map(local, mesh=mesh, in_specs=in_specs, out_specs=out_specs, check_vma=False)
```

```python
import functools

import jax
import jax.numpy as jnp
from jax import lax
from jax.experimental import pallas as pl
from jax.experimental.pallas import tpu as pltpu
from jax.sharding import PartitionSpec as P

F32 = jnp.float32
BF16 = jnp.bfloat16
VMEM_LIMIT = 56 * 1024 * 1024
LANES = 128
COST = 1000
ANY = pl.BlockSpec(memory_space=pl.ANY)


def dot(a, b):
    return jnp.dot(a, b, preferred_element_type=F32)


def dot_rows(a, b):
    return lax.dot_general(a, b, (((0,), (0,)), ((), ())), preferred_element_type=F32)


def dot_columns(a, b):
    return lax.dot_general(a, b, (((1,), (1,)), ((), ())), preferred_element_type=F32)


class Copies:
    def __init__(self, sems):
        self.sems, self.count = sems, 0

    def start(self, src, dst):
        copy = pltpu.make_async_copy(src, dst, self.sems.at[self.count])
        self.count += 1
        copy.start()
        return copy


def forward_kernel(cfg, own_ref, *refs):
    tok, width, ff, experts, cap, top_k, sizes, quarters = cfg
    refs = list(refs)
    take = lambda k: [refs.pop(0) for _ in range(k)]
    pieces = [take(len(sizes)) for _ in range(quarters)]
    (wg, wu, dg, du, wd, dd) = take(6)
    near_hbm, rows_hbm, sel_hbm, grad_hbm, hid_hbm = [take(quarters) for _ in range(5)]
    far_hbm = [take(4) for _ in range(quarters)]
    (x, w, wdv, ddv, rows, sel, pre, grad, hid, out, part, sems) = take(12)
    copies = Copies(sems)
    quarter = sum(sizes) // tok
    n_blocks = quarters * quarter
    per = n_blocks * cap
    of_quarter = per // quarters
    x_in, at = {}, 0
    for q in range(quarters):
        for size, ref in zip(sizes, pieces[q]):
            x_in[at // tok] = copies.start(ref, x.at[pl.ds(at, size)])
            at += size
    w_in, d_in = [], []
    for e in range(experts):
        w_in.append(
            [
                copies.start(src.at[e], w.at[e, :, pl.ds(k * ff, ff)])
                for k, src in enumerate((wg, wu, dg, du))
            ]
        )
        d_in.append([copies.start(wd.at[e], wdv.at[e]), copies.start(dd.at[e], ddv.at[e])])

    before = lax.broadcasted_iota(jnp.int32, (tok, tok), 0) < lax.broadcasted_iota(
        jnp.int32, (tok, tok), 1
    )
    before = before.astype(BF16)
    place = lax.broadcasted_iota(jnp.int32, (cap, tok), 0).astype(F32)
    weight = [[] for _ in range(experts)]
    hits, gates_of = [], []
    for b in range(n_blocks):
        if b in x_in:
            x_in[b].wait()
        routes = x[b * tok : (b + 1) * tok, width : width + LANES].astype(F32).T
        ids = routes[0:top_k]
        gates = (routes[top_k : 2 * top_k] + routes[2 * top_k : 3 * top_k]) + routes[
            3 * top_k : 4 * top_k
        ]
        for e in range(experts):
            named = ids == (own_ref[0] + e).astype(F32)
            hits.append(jnp.sum(jnp.where(named, 1.0, 0.0), axis=0, keepdims=True))
            gates_of.append(jnp.sum(jnp.where(named, gates, 0.0), axis=0, keepdims=True))
    ranks = dot(jnp.concatenate(hits, axis=0).astype(BF16), before)
    for b in range(n_blocks):
        xb = x[b * tok : (b + 1) * tok, :]
        for e in range(experts):
            i = b * experts + e
            chosen = jnp.where((ranks[i : i + 1] == place) & (hits[i] > 0.0), 1.0, 0.0)
            weight[e].append(jnp.sum(chosen * gates_of[i], axis=1, keepdims=True))
            sel[b, e * cap : (e + 1) * cap, :] = chosen.astype(BF16)
        picked = dot(sel[b], xb[:, 0:width]).astype(BF16)
        for e in range(experts):
            rows[e, b * cap : (b + 1) * cap, :] = picked[e * cap : (e + 1) * cap]
    done = []

    def save(src, dst, e):
        for q in range(quarters):
            done.append(
                copies.start(src.at[e, pl.ds(q * of_quarter, of_quarter)], dst[q].at[e])
            )

    for q in range(quarters):
        done.append(copies.start(sel.at[pl.ds(q * quarter, quarter)], sel_hbm[q]))
    for e in range(experts):
        save(rows, rows_hbm, e)

    step = 16
    for e in range(experts):
        for c in w_in[e]:
            c.wait()
        pre[e] = dot(rows[e], w[e])
    for e in range(experts):
        g_all = jnp.concatenate(weight[e], axis=0)
        for r in range(0, per, step):
            at = slice(r, r + step)
            g = g_all[at]
            p, u = pre[e, at, 0:ff], pre[e, at, ff : 2 * ff]
            dgv, duv = pre[e, at, 2 * ff : 3 * ff], pre[e, at, 3 * ff :]
            s = jax.nn.sigmoid(p)
            act = g * (p * s)
            slope = g * (s * (1.0 + p * (1.0 - s)))
            curv = g * (s * (1.0 - s) * (2.0 + p * (1.0 - 2.0 * s)))
            slope_up = slope * u
            hid[e, at, 0:ff] = (act * u).astype(BF16)
            hid[e, at, ff:] = (slope_up * dgv + act * duv).astype(BF16)
            grad[e, at, 0:ff] = slope_up.astype(BF16)
            grad[e, at, ff : 2 * ff] = (curv * dgv * u + slope * duv).astype(BF16)
            grad[e, at, 2 * ff : 3 * ff] = act.astype(BF16)
            grad[e, at, 3 * ff :] = (slope * dgv).astype(BF16)
        save(hid, hid_hbm, e)
        save(grad, grad_hbm, e)
        for c in d_in[e]:
            c.wait()
        h, hd = hid[e, :, 0:ff], hid[e, :, ff:]
        o = dot(h, wdv[e]).astype(BF16)
        od = (dot(hd, wdv[e]) + dot(h, ddv[e])).astype(BF16)
        for b in range(n_blocks):
            out[b, e * cap : (e + 1) * cap, 0:width] = o[b * cap : (b + 1) * cap]
            out[b, e * cap : (e + 1) * cap, width:] = od[b * cap : (b + 1) * cap]
    half = quarter // 2
    for q in reversed(range(quarters)):
        for near in (False, True):
            first = q * quarter + (0 if near else half)
            for b in range(first, first + half):
                part[b * tok : (b + 1) * tok, :] = dot_rows(sel[b], out[b]).astype(BF16)
            if near:
                done.append(copies.start(part.at[pl.ds(first * tok, half * tok)], near_hbm[q]))
                continue
            for y in reversed(range(half)):
                for k in range(2):
                    sent = part.at[pl.ds((first + y) * tok, tok), pl.ds(k * width, width)]
                    done.append(copies.start(sent, far_hbm[q][2 * y + k]))
    for c in done:
        c.wait()


def forward(own, quarters, weights, tok, cap, top_k):
    wg, wd = weights[0], weights[4]
    experts, width, ff = wg.shape
    count = len(quarters)
    sizes = tuple(p.shape[0] for p in quarters[0])
    total = sum(sizes)
    n_blocks = total // tok
    per = n_blocks * cap
    shape = jax.ShapeDtypeStruct
    outs = (
        [shape((total // 2, 2 * width), BF16)] * count
        + [shape((experts, per, width), BF16)] * count
        + [shape((n_blocks, experts * cap, tok), BF16)] * count
        + [shape((experts, per, 4 * ff), BF16)] * count
        + [shape((experts, per, 2 * ff), BF16)] * count
        + [shape((tok, width), BF16)] * (4 * count)
    )
    operands = [p for q in quarters for p in q] + list(weights)
    rows = count * per
    n_sems = count * (len(sizes) + 6 + 3 * experts) + 6 * experts
    flat = pl.pallas_call(
        functools.partial(
            forward_kernel, (tok, width, ff, experts, cap, top_k, sizes, count)
        ),
        in_specs=[pl.BlockSpec(memory_space=pltpu.SMEM)] + [ANY] * len(operands),
        out_specs=[ANY] * len(outs),
        out_shape=outs,
        scratch_shapes=[
            pltpu.VMEM((count * total, quarters[0][0].shape[1]), BF16),
            pltpu.VMEM((experts, width, 4 * ff), BF16),
            pltpu.VMEM((experts, ff, width), BF16),
            pltpu.VMEM((experts, ff, width), BF16),
            pltpu.VMEM((experts, rows, width), BF16),
            pltpu.VMEM((count * n_blocks, experts * cap, tok), BF16),
            pltpu.VMEM((experts, rows, 4 * ff), F32),
            pltpu.VMEM((experts, rows, 4 * ff), BF16),
            pltpu.VMEM((experts, rows, 2 * ff), BF16),
            pltpu.VMEM((count * n_blocks, experts * cap, 2 * width), BF16),
            pltpu.VMEM((count * total, 2 * width), BF16),
            pltpu.SemaphoreType.DMA((n_sems,)),
        ],
        compiler_params=pltpu.CompilerParams(vmem_limit_bytes=VMEM_LIMIT),
        cost_estimate=pl.CostEstimate(
            flops=COST * 2 * experts * rows * width * (7 * ff + 3 * tok) // 100,
            bytes_accessed=COST
            * (2 * count * total * 3 * width + 12 * experts * width * ff)
            // 100,
            transcendentals=0,
        ),
    )(own, *operands)
    far = flat[5 * count :]
    return [[*flat[q : 5 * count : count], far[4 * q : 4 * q + 4]] for q in range(count)]


def grad_kernel(cfg, *refs):
    tok, width, ff, experts, cap, sizes, earlier, last = cfg
    refs = list(refs)
    take = lambda k: [refs.pop(0) for _ in range(k)]
    pieces = [take(len(sizes)) for _ in range(2)]
    sel_hbm, grad_hbm, wd, dd = take(4)
    n_blocks = sum(sizes) // tok
    per = n_blocks * cap
    base = earlier * per
    if last:
        rows_hbm, hid_hbm = take(earlier + 1), take(earlier + 1)
        got_hbm, gud_hbm = take(earlier), take(earlier)
        gate_hbm, up_hbm, down_hbm = take(3)
        rm, sel, grad, wdv, ddv, got, gud, rows, hid, gate, up, down, sems = take(13)
    else:
        got_out, gud_out = take(2)
        rm, sel, grad, wdv, ddv, got, gud, sems = take(8)
    copies = Copies(sems)

    loads = []
    at = 0
    for i, size in enumerate(sizes):
        loads.append([copies.start(p[i], rm.at[k, pl.ds(at, size)]) for k, p in enumerate(pieces)])
        at += size
    first = copies.start(sel_hbm, sel)
    weights = [copies.start(wd, wdv), copies.start(dd, ddv), copies.start(grad_hbm, grad)]
    late = []
    if last:
        for q in range(earlier + 1):
            at = pl.ds(q * per, per)
            for e in range(experts):
                late.append(copies.start(rows_hbm[q].at[e], rows.at[e, at]))
                late.append(copies.start(hid_hbm[q].at[e], hid.at[e, at]))
                if q < earlier:
                    late.append(copies.start(gud_hbm[q].at[e], gud.at[e, at]))
                    for k in range(2):
                        late.append(copies.start(got_hbm[q].at[k, e], got.at[k, e, at]))
    first.wait()
    at = 0
    for i, size in enumerate(sizes):
        for c in loads[i]:
            c.wait()
        for b in range(at // tok, (at + size) // tok):
            for k in range(2):
                picked = dot(sel[b], rm[k, b * tok : (b + 1) * tok, :]).astype(BF16)
                for e in range(experts):
                    to = base + b * cap
                    got[k, e, to : to + cap, :] = picked[e * cap : (e + 1) * cap]
        at += size
    for c in weights:
        c.wait()
    done = []
    if not last:
        done.append(copies.start(got, got_out))
    step = 16
    for e in range(experts):
        r, m = got[0, e, base : base + per, :], got[1, e, base : base + per, :]
        grad_h = dot_columns(r, wdv[e])
        grad_d = dot_columns(m, wdv[e]) + dot_columns(r, ddv[e])
        for k in range(0, per, step):
            at, to = slice(k, k + step), slice(base + k, base + k + step)
            gh, gd = grad_h[at], grad_d[at]
            part = lambda i: grad[e, at, i * ff : (i + 1) * ff].astype(F32)
            gud[e, to, 0:ff] = (gd * part(0) + gh * part(1)).astype(BF16)
            gud[e, to, ff:] = (gd * part(2) + gh * part(3)).astype(BF16)
    if not last:
        done.append(copies.start(gud, gud_out))
    else:
        for c in late:
            c.wait()
        for e in range(experts):
            d = dot_rows(hid[e, :, ff:], got[0, e]) + dot_rows(hid[e, :, 0:ff], got[1, e])
            down[e] = d.astype(BF16)
            done.append(copies.start(down.at[e], down_hbm.at[e]))
            gu = dot_rows(rows[e], gud[e]).astype(BF16)
            gate[e] = gu[:, 0:ff]
            up[e] = gu[:, ff:]
            done.append(copies.start(gate.at[e], gate_hbm.at[e]))
            done.append(copies.start(up.at[e], up_hbm.at[e]))
    for c in done:
        c.wait()


def backward(r_pieces, m_pieces, saved, wd, dd, tok, cap, before=()):
    experts, ff, width = wd.shape
    last = len(before) > 0
    earlier = len(before)
    sizes = tuple(p.shape[0] for p in r_pieces)
    total = sum(sizes)
    n_blocks = total // tok
    per = n_blocks * cap
    count = (earlier + 1) * per
    shape = jax.ShapeDtypeStruct
    d = (experts, ff, width)
    _, sel, grad, _ = saved[-1]
    operands = [*r_pieces, *m_pieces, sel, grad, wd, dd]
    scratch = [
        pltpu.VMEM((2, total, width), BF16),
        pltpu.VMEM((n_blocks, experts * cap, tok), BF16),
        pltpu.VMEM((experts, per, 4 * ff), BF16),
        pltpu.VMEM(d, BF16),
        pltpu.VMEM(d, BF16),
        pltpu.VMEM((2, experts, count, width), BF16),
        pltpu.VMEM((experts, count, 2 * ff), BF16),
    ]
    n_sems = 2 * len(sizes) + 4
    if last:
        operands += [s[0] for s in saved] + [s[3] for s in saved]
        operands += [b[0] for b in before] + [b[1] for b in before]
        outs = [shape((experts, width, ff), BF16)] * 2 + [shape(d, BF16)]
        scratch += [pltpu.VMEM((experts, count, width), BF16), pltpu.VMEM((experts, count, 2 * ff), BF16)]
        scratch += [pltpu.VMEM(o.shape, BF16) for o in outs]
        n_sems += experts * (2 + 5 * earlier) + 3 * experts
        macs = experts * count * width * 4 * ff
    else:
        outs = [
            shape((2, experts, per, width), BF16),
            shape((experts, per, 2 * ff), BF16),
        ]
        n_sems += 2
        macs = 0
    return pl.pallas_call(
        functools.partial(
            grad_kernel, (tok, width, ff, experts, cap, sizes, earlier, last)
        ),
        in_specs=[ANY] * len(operands),
        out_specs=[ANY] * len(outs),
        out_shape=outs,
        scratch_shapes=scratch + [pltpu.SemaphoreType.DMA((n_sems,))],
        compiler_params=pltpu.CompilerParams(vmem_limit_bytes=VMEM_LIMIT),
        cost_estimate=pl.CostEstimate(
            flops=COST * 2 * (experts * per * width * (3 * ff + 2 * tok) + macs) // 100,
            bytes_accessed=COST * (2 * total * 3 * width + 4 * experts * width * ff) // 100,
            transcendentals=0,
        ),
    )(*operands)


def local(
    tokens, target, expert_ids, gate_weights, w_gate, w_up, w_down, dir_gate, dir_up, dir_down
):
    n = lax.axis_size("expert")
    me = lax.axis_index("expert")
    nz = n // 4
    experts, width, ff = w_gate.shape
    tok, top_k = expert_ids.shape
    capacity = max(2, 3 * tok * top_k // (2 * experts * n))
    cap = -(-capacity // 16) * 16

    def send(x, to):
        return lax.ppermute(x, "expert", [(i, to(i)) for i in range(n)])

    ahead = lambda x: send(x, lambda i: (i + 4) % n)
    side = lambda x: send(x, lambda i: i ^ 2)
    core = lambda x: send(x, lambda i: i ^ 1)

    def add(a, b):
        return a.astype(F32) + b.astype(F32)

    def after(x, *others):
        return lax.optimization_barrier((x, *others))[0]

    def gather(x):
        steps = []
        for d in range(nz):
            if d:
                x = ahead(x)
            steps.append((x, side(x)))
        return steps

    exact = lambda a: lax.reduce_precision(a, 8, 7)
    high = exact(gate_weights)
    middle = exact(gate_weights - high)
    low = gate_weights - high - middle
    routes = jnp.concatenate([expert_ids.astype(F32), high, middle, low], 1).astype(BF16)
    routes = jnp.pad(routes, ((0, 0), (0, LANES - 4 * top_k)))
    own = (me * experts).astype(jnp.int32).reshape(1)
    weights = (w_gate, w_up, dir_gate, dir_up, w_down, dir_down)

    cols = (slice(0, width), slice(width, 2 * width))
    half = nz // 2
    saved = []
    mine, other, over = ([], []), ([], []), ([], [])
    a = jnp.concatenate([tokens, routes], 1)
    ring = [a]
    for d in range(1, nz):
        ring.append(ahead(ring[-1]))
    sides = [side(a) for a in ring[: half + 1]]
    for first, last in ((0, half), (half, nz)):
        start = own
        if first == 0:
            start = after(own, ring[min(half, nz - 1)])
        else:
            start = after(own, other[0][1])
            for d in range(half + 1, nz):
                sides.append(side(after(ring[d], saved[0][1], sides[half])))
        quarters = [(ring[d], sides[d], core(ring[d]), core(sides[d])) for d in range(first, last)]
        for d, (near, *rest, far) in enumerate(
            forward(start, quarters, weights, tok, cap, top_k), first
        ):
            saved.append(rest)
            for k, c in enumerate(cols):
                f = far[2 + k]
                if first:
                    f = after(f, over[k][1])
                o = add(near[tok:, c], core(f)).astype(BF16)
                other[k].append(o)
                over[k].append(side(o))
            for k, c in enumerate(cols):
                mine[k].append(add(near[0:tok, c], core(far[k])))

    def ring_sum(k, then=None):
        total = None
        for d in [*range(1, nz), 0]:
            s = add(mine[k][d], over[k][d])
            if total is not None:
                t = total.astype(BF16)
                if d == 0 and then is not None:
                    t = after(t, then)
                s = s + ahead(t).astype(F32)
            total = s
        return total

    r = gather((ring_sum(0) - target.astype(F32)).astype(BF16))
    ma = ring_sum(1, r[0][0]).astype(BF16)
    mb = side(ma)
    before, nexts = [], [ahead(ma)]
    for d in range(nz):
        (ra, rb) = r[d]
        last_b = after(mb, before[-1][1]) if d == nz - 1 else mb
        pieces = (ra, rb, core(ra), core(rb)), (ma, mb, core(ma), core(last_b))
        if d == nz - 1:
            break
        pieces = ((after(ra, nexts[d]), *pieces[0][1:]), pieces[1])
        before.append(backward(*pieces, saved[d : d + 1], w_down, dir_down, tok, cap))
        ma = nexts[d]
        if d + 2 < nz:
            nexts.append(ahead(ma))
            nexts[d + 1] = after(nexts[d + 1], before[d][1])
        mb = side(ma)
    return tuple(backward(*pieces, saved, w_down, dir_down, tok, cap, before=before))


def solution(mesh):
    in_specs = (
        P(("groups", "expert"), None),
        P(("groups", "expert"), None),
        P(("groups", "expert"), None),
        P(("groups", "expert"), None),
        P("expert", None, None),
        P("expert", None, None),
        P("expert", None, None),
        P("expert", None, None),
        P("expert", None, None),
        P("expert", None, None),
    )
    out_specs = (
        P(("groups", "expert"), None, None),
        P(("groups", "expert"), None, None),
        P(("groups", "expert"), None, None),
    )
    return jax.shard_map(local, mesh=mesh, in_specs=in_specs, out_specs=out_specs, check_vma=False)
```
